32 devices in a mesh: wide: 8 (over y, x, core), narrow: 4 (over z).
Axes of the slice: x: 2, y: 2, z: 4, core: 2. Of those that a mesh axis runs over, the one named last changes fastest.
Arguments:
- inputs: float32 [16, 2048, 768], P('wide', 'narrow'), may hold values from -6 to 6
- cotangent: bfloat16 [16, 2048, 768], P('wide', 'narrow'), may hold values from -6 to 6
- w_qkv: bfloat16 [768, 2304], replicated, may hold values from -0.21875 to 0.21875
- w_out: bfloat16 [768, 768], replicated, may hold values from -3.5 to 3.5
- w_up: bfloat16 [768, 3072], replicated, may hold values from -0.21875 to 0.21875
- w_down: bfloat16 [3072, 768], replicated, may hold values from -0.109375 to 0.109375
- router_weight: float32 [768], replicated, may hold values from -0.21875 to 0.21875
- gain_attn: float32 [768], replicated, may hold values from 0.1 to 1.9
- gain_mlp: float32 [768], replicated, may hold values from 0.1 to 1.9
- sel_idx: int32 [16, 512], P('wide'), may hold values from 0 to 2047, as said below
- sel_count: int32 [16], P('wide'), may hold values from 2 to 512, as said below
Outputs:
- output: float32 [16, 2048, 768], P('wide', 'narrow')
- grad_inputs: float32 [16, 2048, 768], P('wide', 'narrow')
- grad_w_qkv: float32 [768, 2304], P('wide')
- grad_w_out: float32 [768, 768], P('wide')
- grad_w_up: float32 [768, 3072], P('wide')
- grad_w_down: float32 [3072, 768], P('wide')
- grad_router_weight: float32 [768], replicated
- grad_gain_attn: float32 [768], replicated
- grad_gain_mlp: float32 [768], replicated
The draws below stay inside these ranges and needn't reach their ends.
Inputs may be any that keep to these rules, and one draw needn't show every extreme that they name: `sel_idx`: in each row the first sel_count entries are that sequence's selected positions in rising order; the remaining entries are other positions of the sequence in rising order; all entries of a row differ. At most 256 selected positions of a sequence lie in one aligned block of 512 positions, and in every draw some block of some sequence holds exactly 256. sel_count equals the number of selected positions of the sequence; some sequence has exactly 512.
All inputs are finite; a program needn't handle non-finite values.
Results may differ from the reference program's by a relative error of at most 0.012.
Values may be sent and summed in bfloat16 or wider, within the bound.
A program may use at most 448 MiB of HBM per device.

```python
import jax
import jax.numpy as jnp
from jax import lax

D = 768
HEADS = 12
HEAD_DIM = 64
FF = 3072
LENGTH = 2048
TOK_DEV = 512
BLOCK_MOST = 256
KMAX = 512
SEQUENCES = 16
N_NARROW = 4


def selection(key):
    first_key, second_key, heavy_key, pair_key, swap_key, order_key = jax.random.split(key, 6)
    pairs = N_NARROW // 2
    first = jax.random.randint(first_key, (SEQUENCES, pairs), 1, BLOCK_MOST + 1)
    second = jax.random.randint(second_key, (SEQUENCES, pairs), 0, BLOCK_MOST + 1) % (BLOCK_MOST - first + 1)
    heavy = jax.random.randint(heavy_key, (), 0, SEQUENCES)
    heavy_pair = jax.random.randint(pair_key, (), 0, pairs)
    is_heavy = jnp.arange(SEQUENCES)[:, None] == heavy
    first = jnp.where(is_heavy & (jnp.arange(pairs)[None, :] == heavy_pair), BLOCK_MOST, first)
    second = jnp.where(is_heavy, BLOCK_MOST - first, second)
    swapped = jax.random.randint(swap_key, (SEQUENCES, pairs), 0, 2) == 1
    lower = jnp.where(swapped, second, first)
    higher = jnp.where(swapped, first, second)
    per_block = jnp.stack([lower, higher], -1).reshape(SEQUENCES, N_NARROW)
    row_keys = jax.random.split(order_key, SEQUENCES * N_NARROW)
    orders = jax.vmap(lambda row_key: jax.random.permutation(row_key, TOK_DEV))(row_keys)
    orders = orders.reshape(SEQUENCES, N_NARROW, TOK_DEV)
    ranks = jnp.arange(TOK_DEV)[None, None, :]
    positions = orders + jnp.arange(N_NARROW)[None, :, None] * TOK_DEV
    chosen = ranks < per_block[:, :, None]
    ordering = jnp.where(chosen, positions, positions + LENGTH).reshape(SEQUENCES, LENGTH)
    ordered = jnp.sort(ordering, axis=-1)[:, :KMAX]
    ordered = jnp.where(ordered >= LENGTH, ordered - LENGTH, ordered)
    return (ordered.astype(jnp.int32), jnp.sum(per_block, -1).astype(jnp.int32))


def draw_sel_idx(key, part):
    return selection(key)[0]


def draw_sel_count(key, part):
    return selection(key)[1]


def strengthened(drawn, key, source, target, parts, factor):
    owner, partner = [(jnp.arange(drawn.shape[dim]) // (drawn.shape[dim] // parts)).reshape([-1 if axis == dim else 1 for axis in range(drawn.ndim)]) for dim in (source, target)]
    chosen = jax.random.permutation(key, parts)[partner]
    strong = (owner == chosen) | (owner == (partner + parts // 2) % parts)
    return jnp.where(strong, factor * drawn, drawn)


def levels(key, shape, pieces, least, top_value):
    def one(position, parts):
        steps = jax.random.uniform(jax.random.fold_in(jax.random.fold_in(key, 6), position), (parts,), jnp.float32, least / len(pieces), top_value / len(pieces))
        return jnp.repeat(jnp.exp(steps), shape[position] // parts).reshape((-1,) + (1,) * (len(shape) - position - 1))

    level = one(*pieces[0])
    for cut in pieces[1:]:
        level = level * one(*cut)
    return level


def centred(own_key, dims, scale, limit, pieces=(), kind=jnp.bfloat16):
    level = levels(own_key, dims, pieces, -0.22, 0.18) if pieces else 1.0
    values = jax.random.normal(own_key, dims, jnp.float32) * scale * level
    return jnp.minimum(jnp.maximum(values, -limit), limit).astype(kind)


def noise_with(stream_key, shape, deviation, bound, cuts, heavy, kind=jnp.bfloat16):
    values = deviation * jax.random.normal(stream_key, shape, jnp.float32)
    if cuts:
        values = values * levels(stream_key, shape, cuts, -0.22, 0.18)
    return jnp.clip(strengthened(values, jax.random.fold_in(stream_key, 3), *heavy), -bound, bound).astype(kind)


def setup_inputs(seed: int = 0) -> dict:
    seeds = jax.random.split(jax.random.key(seed), 12)
    return {
        "inputs": noise_with(seeds[0], (SEQUENCES, LENGTH, D), 1.0, 6.0, ((0, 8), (1, 4)), (0, 2, 8, 2.0), jnp.float32),
        "cotangent": centred(seeds[1], (SEQUENCES, LENGTH, D), 1.0, 6.0, ((0, 8), (1, 4))),
        "w_qkv": centred(seeds[2], (D, 3 * D), D ** -0.5, 0.21875),
        "w_out": centred(seeds[3], (D, D), (max(1, D // 256)) ** -0.5, 3.5),
        "w_up": centred(seeds[4], (D, FF), D ** -0.5, 0.21875),
        "w_down": centred(seeds[5], (FF, D), FF ** -0.5, 0.109375),
        "router_weight": centred(seeds[6], (D,), D ** -0.5, 0.21875, (), jnp.float32),
        "gain_attn": jnp.clip(1.0 + 0.18 * jax.random.normal(seeds[7], (D,), jnp.float32), 0.1, 1.9),
        "gain_mlp": jnp.clip(1.0 + 0.18 * jax.random.normal(seeds[8], (D,), jnp.float32), 0.1, 1.9),
        "sel_idx": draw_sel_idx(jax.random.fold_in(seeds[11], 71), 0),
        "sel_count": draw_sel_count(jax.random.fold_in(seeds[11], 71), 0),
    }


EPSILON = 1e-06
HIGHEST = lax.Precision.HIGHEST

@jax.custom_vjp
def low(v):
    return lax.optimization_barrier(v.astype(jnp.bfloat16)).astype(jnp.float32)

@jax.custom_vjp
def low_back(v):
    return v

def low_keep(v):
    return (low(v), None)

def low_pass(kept, grad):
    return (grad,)

def back_keep(v):
    return (v, None)

def back_low(kept, grad):
    return (low(grad),)
low.defvjp(low_keep, low_pass)
low_back.defvjp(back_keep, back_low)

def normed(values, gain):
    return values * lax.rsqrt(lax.optimization_barrier(jnp.mean(values * values, -1, keepdims=True)) + EPSILON) * gain

def attention(queries, keyset, valueset):
    block_rows = min(512, queries.shape[0])
    blocks = queries.shape[0] // block_rows
    score_scale = HEAD_DIM ** (-0.5)
    key_places = jnp.arange(keyset.shape[0])

    @jax.checkpoint
    def one_block(member):
        query_block, first_row = member
        scores = jnp.einsum('qhd,khd->hqk', query_block, keyset, precision=HIGHEST) * score_scale
        scores = low_back(scores)
        query_places = first_row + jnp.arange(block_rows)
        allowed = key_places[None, None, :] <= query_places[None, :, None]
        scores = jnp.where(allowed, scores, -1e+30)
        peak = lax.optimization_barrier(jnp.max(scores, -1, keepdims=True))
        expo = jnp.exp(scores - peak)
        probs = low(expo / lax.optimization_barrier(jnp.sum(expo, -1, keepdims=True)))
        return jnp.einsum('hqk,khd->qhd', probs, valueset, precision=HIGHEST)
    firsts = jnp.arange(blocks) * block_rows
    result = lax.map(one_block, (queries.reshape(blocks, block_rows, HEADS, HEAD_DIM), firsts))
    return result.reshape(queries.shape[0], HEADS * HEAD_DIM)

def block_layer(values, wqkv, wout, wup, wdown, router_w, gain_one, gain_two, positions, amount):
    width = values.shape[-1]
    seq_len = values.shape[0]
    normed_in = low(normed(values, gain_one))
    packed = low(low_back(jnp.dot(normed_in, wqkv, precision=HIGHEST)))
    queries = packed[:, :width].reshape(seq_len, HEADS, HEAD_DIM)
    keyset = packed[:, width:2 * width].reshape(seq_len, HEADS, HEAD_DIM)
    valueset = packed[:, 2 * width:].reshape(seq_len, HEADS, HEAD_DIM)
    mixed = low(low_back(attention(queries, keyset, valueset)))
    resid = values + low_back(jnp.dot(mixed, wout, precision=HIGHEST))
    router = lax.optimization_barrier(jnp.sum(resid * router_w, -1))
    valid = (jnp.arange(positions.shape[0]) < amount).astype(values.dtype)
    picked = resid[positions]
    rows_low = low(low_back(normed(picked, gain_two)))
    upper = low_back(jnp.dot(rows_low, wup, precision=HIGHEST))
    hidden = low(jax.nn.gelu(upper, approximate=False))
    branch = low(low_back(jnp.dot(hidden, wdown, precision=HIGHEST)))
    return resid.at[positions].add((valid * router[positions])[:, None] * branch)

def reference(inputs, cotangent, w_qkv, w_out, w_up, w_down, router_weight, gain_attn, gain_mlp, sel_idx, sel_count):
    weights = (w_qkv.astype(jnp.float32), w_out.astype(jnp.float32), w_up.astype(jnp.float32), w_down.astype(jnp.float32), router_weight.astype(jnp.float32), gain_attn.astype(jnp.float32), gain_mlp.astype(jnp.float32))

    def per_sequence(running, member):
        seq_input, seq_cot, seq_positions, seq_amount = member

        def forward(values, *params):
            return block_layer(values, *params, seq_positions, seq_amount)
        result, pullback = jax.vjp(forward, seq_input, *weights)
        grads = pullback(seq_cot.astype(jnp.float32))
        running = tuple((before + update for before, update in zip(running, grads[1:])))
        return (running, (result, grads[0]))
    zeros = tuple((jnp.zeros_like(tensor) for tensor in weights))
    totals, (outputs, grad_inputs) = lax.scan(per_sequence, zeros, (inputs, cotangent, sel_idx, sel_count))
    return (outputs, grad_inputs, totals[0], totals[1], totals[2], totals[3], totals[4], totals[5], totals[6])
```

```python
from functools import partial

import jax
import jax.numpy as jnp
from jax import lax
from jax.experimental import pallas as pl
from jax.experimental.pallas import tpu as pltpu
from jax.sharding import PartitionSpec as P

HEADS = 12
HEAD_DIM = 64
EPSILON = 1e-06
MESH = pl.DeviceIdType.MESH
LOW = jnp.bfloat16
HIGHEST = lax.Precision.HIGHEST
VMEM_MOST = 56 * 1024 * 1024


def matmul(left, right):
    return jnp.dot(left, right, preferred_element_type=jnp.float32)


def dot_dims(left, right, left_dim, right_dim, precision=None):
    return lax.dot_general(
        left,
        right,
        (((left_dim,), (right_dim,)), ((), ())),
        precision=precision,
        preferred_element_type=jnp.float32,
    )


class Place:
    def __init__(self, narrow_size, seqs):
        self.narrow_size = narrow_size
        self.span = max(1, 8 // narrow_size)
        self.seqs = seqs
        self.members = self.span * narrow_size
        self.team = self.members // (seqs * self.span)

    def locate(self):
        wide, narrow = lax.axis_index("wide"), lax.axis_index("narrow")
        self.narrow = narrow
        self.offset = lax.rem(wide, self.span)
        self.group = wide // self.span
        self.me = narrow * self.span + self.offset
        self.seq = self.me // self.team
        self.rank = lax.rem(self.me, self.team)
        return self

    def device(self, member):
        return {
            "wide": self.group * self.span + lax.rem(member, self.span),
            "narrow": member // self.span,
        }

    def sibling(self, step):
        return self.seq * self.team + lax.rem(self.rank + step, self.team)

    def greet_group(self):
        barrier = pltpu.get_barrier_semaphore()
        for step in range(1, self.members):
            other = lax.rem(self.me + step, self.members)
            pl.semaphore_signal(
                barrier, inc=1, device_id=self.device(other), device_id_type=MESH
            )
        pl.semaphore_wait(barrier, self.members - 1)

    def greet_team(self):
        barrier = pltpu.get_barrier_semaphore()
        for step in range(1, self.team):
            pl.semaphore_signal(
                barrier, inc=1, device_id=self.device(self.sibling(step)), device_id_type=MESH
            )
        pl.semaphore_wait(barrier, self.team - 1)


def remote(src, dst, send, recv, device):
    return pltpu.make_async_remote_copy(
        src_ref=src, dst_ref=dst, send_sem=send, recv_sem=recv, device_id=device, device_id_type=MESH
    )


def spread_start(place, src, dst, sems):
    send, recv, fsend, frecv, local = sems
    rows = src.shape[1]
    part = rows // place.team
    for seq in range(place.seqs):
        for rank in range(place.team):
            target = (place.seqs * place.offset + seq) * place.team + rank
            source_rows = src.at[seq, pl.ds(rank * part, part)]
            start = pl.multiple_of(place.narrow * rows + rank * part, part)
            landing = dst.at[pl.ds(start, part)]

            @pl.when(target == place.me)
            def _():
                pltpu.make_async_copy(source_rows, landing, local).start()

            @pl.when(target != place.me)
            def _():
                remote(
                    source_rows,
                    landing,
                    send.at[seq, rank],
                    recv.at[place.narrow],
                    place.device(target),
                ).start()


def spread_finish(place, src, dst, sems):
    send, recv, fsend, frecv, local = sems
    rows = src.shape[1]
    part = rows // place.team

    def landed(block, rank):
        return dst.at[pl.ds(pl.multiple_of(block * rows + rank * part, part), part)]

    for block in range(place.narrow_size):
        source = block * place.span + place.seq // place.seqs
        mine = landed(block, place.rank)

        @pl.when(source == place.me)
        def _():
            pltpu.make_async_copy(mine, mine, local).wait()

        @pl.when(source != place.me)
        def _():
            remote(
                mine, mine, send.at[0, 0], recv.at[block], place.device(place.sibling(1))
            ).wait_recv()

        for step in range(1, place.team):
            remote(
                mine,
                mine,
                fsend.at[block, step - 1],
                frecv.at[block, step - 1],
                place.device(place.sibling(step)),
            ).start()
    for block in range(place.narrow_size):
        for step in range(1, place.team):
            other = lax.rem(place.rank + place.team - step, place.team)
            theirs = landed(block, other)
            copy = remote(
                landed(block, place.rank),
                theirs,
                fsend.at[block, step - 1],
                frecv.at[block, step - 1],
                place.device(place.sibling(step)),
            )
            copy.wait_send()
            copy.wait_recv()
    for seq in range(place.seqs):
        for rank in range(place.team):
            target = (place.seqs * place.offset + seq) * place.team + rank

            @pl.when(target != place.me)
            def _():
                source_rows = src.at[seq, pl.ds(rank * part, part)]
                remote(
                    source_rows,
                    source_rows,
                    send.at[seq, rank],
                    recv.at[0],
                    place.device(target),
                ).wait_send()


def spread_sems(place):
    return [
        pltpu.SemaphoreType.DMA((place.seqs, place.team)),
        pltpu.SemaphoreType.DMA((place.narrow_size,)),
        pltpu.SemaphoreType.DMA((place.narrow_size, place.team - 1)),
        pltpu.SemaphoreType.DMA((place.narrow_size, place.team - 1)),
        pltpu.SemaphoreType.DMA(()),
    ]


def spread_kernel(place, x_ref, c_ref, f_ref, l_ref, xs_ref, cs_ref, fs_ref, ls_ref, *sems):
    lsend, lrecv, llocal, rsend, rrecv, rlocal = sems[:6]
    sems = sems[6:]
    place.locate()
    place.greet_group()
    own = ls_ref.at[place.offset]
    pltpu.make_async_copy(l_ref, own, llocal).start()
    for step in range(1, place.span):
        other = place.narrow * place.span + lax.rem(place.offset + step, place.span)
        remote(l_ref, own, lsend.at[step - 1], lrecv.at[step - 1], place.device(other)).start()

    def factors(act_local, act_remote):
        for seq in range(place.seqs):
            for rank in range(place.team):
                target = (place.seqs * place.offset + seq) * place.team + rank

                @pl.when(target == place.me)
                def _():
                    act_local(
                        pltpu.make_async_copy(f_ref.at[seq], fs_ref.at[place.narrow], rlocal)
                    )

                @pl.when(target != place.me)
                def _():
                    act_remote(
                        remote(
                            f_ref.at[seq],
                            fs_ref.at[place.narrow],
                            rsend.at[seq, rank],
                            rrecv.at[place.narrow],
                            place.device(target),
                        )
                    )

    factors(lambda copy: copy.start(), lambda copy: copy.start())
    spread_start(place, x_ref, xs_ref, sems[:5])
    spread_start(place, c_ref, cs_ref, sems[5:])
    for step in range(1, place.span):
        back = lax.rem(place.offset + place.span - step, place.span)
        other = place.narrow * place.span + lax.rem(place.offset + step, place.span)
        copy = remote(
            l_ref, ls_ref.at[back], lsend.at[step - 1], lrecv.at[step - 1], place.device(other)
        )
        copy.wait_send()
        copy.wait_recv()
    pltpu.make_async_copy(l_ref, own, llocal).wait()
    factors(lambda copy: copy.wait(), lambda copy: copy.wait_send())
    for block in range(place.narrow_size):
        source = block * place.span + place.seq // place.seqs

        @pl.when(source != place.me)
        def _():
            remote(
                f_ref.at[0],
                fs_ref.at[block],
                rsend.at[0, 0],
                rrecv.at[block],
                place.device(place.sibling(1)),
            ).wait_recv()

    spread_finish(place, x_ref, xs_ref, sems[:5])
    spread_finish(place, c_ref, cs_ref, sems[5:])


def spread(place, rows_low, cotangent, factors, lists, collective_id):
    seqs, rows, width = rows_low.shape
    full = jax.ShapeDtypeStruct((place.narrow_size * rows, width), LOW)
    anywhere = pl.BlockSpec(memory_space=pl.ANY)
    inside = pl.BlockSpec(memory_space=pltpu.VMEM)
    steps = max(1, place.span - 1)
    return pl.pallas_call(
        partial(spread_kernel, place),
        out_shape=(
            full,
            full,
            jax.ShapeDtypeStruct((place.narrow_size,) + factors.shape[1:], factors.dtype),
            jax.ShapeDtypeStruct((place.span,) + lists.shape, lists.dtype),
        ),
        in_specs=[inside] * 4,
        out_specs=(anywhere,) * 4,
        scratch_shapes=[
            pltpu.SemaphoreType.DMA((steps,)),
            pltpu.SemaphoreType.DMA((steps,)),
            pltpu.SemaphoreType.DMA(()),
            pltpu.SemaphoreType.DMA((place.seqs, place.team)),
            pltpu.SemaphoreType.DMA((place.narrow_size,)),
            pltpu.SemaphoreType.DMA(()),
        ]
        + spread_sems(place)
        + spread_sems(place),
        compiler_params=pltpu.CompilerParams(
            collective_id=collective_id, has_side_effects=True, vmem_limit_bytes=VMEM_MOST
        ),
        name="spread_rows",
    )(rows_low, cotangent, factors, lists)


def share_kernel(place, x_ref, out_ref, send, recv, local):
    place.locate()
    place.greet_team()
    own = out_ref.at[place.rank]
    pltpu.make_async_copy(x_ref, own, local).start()
    for step in range(1, place.team):
        remote(
            x_ref, own, send.at[step - 1], recv.at[step - 1], place.device(place.sibling(step))
        ).start()
    for step in range(1, place.team):
        back = lax.rem(place.rank + place.team - step, place.team)
        copy = remote(
            x_ref,
            out_ref.at[back],
            send.at[step - 1],
            recv.at[step - 1],
            place.device(place.sibling(step)),
        )
        copy.wait_send()
        copy.wait_recv()
    pltpu.make_async_copy(x_ref, own, local).wait()


def share(place, part, collective_id):
    anywhere = pl.BlockSpec(memory_space=pl.ANY)
    return pl.pallas_call(
        partial(share_kernel, place),
        out_shape=jax.ShapeDtypeStruct((place.team,) + part.shape, part.dtype),
        in_specs=[pl.BlockSpec(memory_space=pltpu.VMEM)],
        out_specs=anywhere,
        scratch_shapes=[
            pltpu.SemaphoreType.DMA((place.team - 1,)),
            pltpu.SemaphoreType.DMA((place.team - 1,)),
            pltpu.SemaphoreType.DMA(()),
        ],
        compiler_params=pltpu.CompilerParams(
            collective_id=collective_id, has_side_effects=True, vmem_limit_bytes=VMEM_MOST
        ),
        name="share_parts",
    )(part)


def split_kernel(place, x_ref, out_ref, send, recv, local):
    place.locate()
    place.greet_team()
    rows = x_ref.shape[0] // place.team

    def rows_of(rank):
        return x_ref.at[pl.ds(pl.multiple_of(rank * rows, rows), rows)]

    pltpu.make_async_copy(rows_of(place.rank), out_ref.at[0], local).start()
    for step in range(1, place.team):
        target = lax.rem(place.rank + step, place.team)
        remote(
            rows_of(target),
            out_ref.at[step],
            send.at[step - 1],
            recv.at[step - 1],
            place.device(place.sibling(step)),
        ).start()
    for step in range(1, place.team):
        target = lax.rem(place.rank + step, place.team)
        copy = remote(
            rows_of(target),
            out_ref.at[step],
            send.at[step - 1],
            recv.at[step - 1],
            place.device(place.sibling(step)),
        )
        copy.wait_send()
        copy.wait_recv()
    pltpu.make_async_copy(rows_of(place.rank), out_ref.at[0], local).wait()


def split(place, terms, collective_id):
    anywhere = pl.BlockSpec(memory_space=pl.ANY)
    rows, width = terms.shape
    return pl.pallas_call(
        partial(split_kernel, place),
        out_shape=jax.ShapeDtypeStruct((place.team, rows // place.team, width), terms.dtype),
        in_specs=[pl.BlockSpec(memory_space=pltpu.VMEM)],
        out_specs=anywhere,
        scratch_shapes=[
            pltpu.SemaphoreType.DMA((place.team - 1,)),
            pltpu.SemaphoreType.DMA((place.team - 1,)),
            pltpu.SemaphoreType.DMA(()),
        ],
        compiler_params=pltpu.CompilerParams(
            collective_id=collective_id, has_side_effects=True, vmem_limit_bytes=VMEM_MOST
        ),
        name="split_terms",
    )(terms)


def give_back_kernel(place, *refs):
    count = (len(refs) - 3) // 2
    sources, results = refs[:count], refs[count : 2 * count]
    send, recv, local = refs[2 * count :]
    place.locate()
    place.greet_group()
    rows = results[0].shape[1]
    blocks = place.narrow_size // place.team

    def each(act):
        for item, (src, dst) in enumerate(zip(sources, results)):
            for index in range(blocks):
                block = place.rank * blocks + index
                target = block * place.span + place.seq // place.seqs
                seq = lax.rem(place.seq, place.seqs)
                act(item, index, src.at[pl.ds(index * rows, rows)], dst.at[seq], seq, target)

    def begin(item, index, rows_here, landing, seq, target):
        @pl.when(target == place.me)
        def _():
            pltpu.make_async_copy(rows_here, landing, local.at[item, index]).start()

        @pl.when(target != place.me)
        def _():
            remote(
                rows_here,
                landing,
                send.at[item, index],
                recv.at[item, seq],
                place.device(target),
            ).start()

    def end(item, index, rows_here, landing, seq, target):
        @pl.when(target == place.me)
        def _():
            pltpu.make_async_copy(rows_here, landing, local.at[item, index]).wait()

        @pl.when(target != place.me)
        def _():
            remote(
                rows_here,
                landing,
                send.at[item, index],
                recv.at[item, seq],
                place.device(target),
            ).wait_send()

    each(begin)
    for item, dst in enumerate(results):
        for seq in range(place.seqs):
            source = (place.seqs * place.offset + seq) * place.team + place.narrow // blocks

            @pl.when(source != place.me)
            def _():
                remote(
                    dst.at[seq],
                    dst.at[seq],
                    send.at[0, 0],
                    recv.at[item, seq],
                    place.device(source),
                ).wait_recv()

    each(end)


def give_back(place, arrays, collective_id):
    anywhere = pl.BlockSpec(memory_space=pl.ANY)
    blocks = place.narrow_size // place.team
    rows, width = arrays[0].shape
    count = len(arrays)
    return pl.pallas_call(
        partial(give_back_kernel, place),
        out_shape=tuple(
            jax.ShapeDtypeStruct((place.seqs, rows // blocks, width), a.dtype) for a in arrays
        ),
        in_specs=[pl.BlockSpec(memory_space=pltpu.VMEM)] * count,
        out_specs=(anywhere,) * count,
        scratch_shapes=[
            pltpu.SemaphoreType.DMA((count, blocks)),
            pltpu.SemaphoreType.DMA((count, place.seqs)),
            pltpu.SemaphoreType.DMA((count, blocks)),
        ],
        compiler_params=pltpu.CompilerParams(
            collective_id=collective_id, has_side_effects=True, vmem_limit_bytes=VMEM_MOST
        ),
        name="give_back_rows",
    )(*arrays)


def half_lanes(half, shape):
    lane = lax.broadcasted_iota(jnp.int32, shape, len(shape) - 1)
    return (lane // HEAD_DIM) == half


def only_half(values, half):
    return jnp.where(half_lanes(half, values.shape), values, jnp.zeros_like(values))


def attend_kernel(block, q_ref, k_ref, v_ref, o_ref, lse_ref):
    here = pl.program_id(1)
    pair = q_ref[...]
    width = pair.shape[1]
    ones = jnp.ones((block, width), LOW)
    rows = lax.broadcasted_iota(jnp.int32, (block, block), 0)
    cols = lax.broadcasted_iota(jnp.int32, (block, block), 1)
    total = jnp.zeros((block, width), jnp.float32)
    for half in range(2):
        query = only_half(pair, half)

        def step(index, carry, masked):
            peak, acc = carry
            place = pl.ds(pl.multiple_of(index * block, block), block)
            scores = dot_dims(query, k_ref[place, :], 1, 1)
            if masked:
                scores = jnp.where(cols <= rows, scores, -1e30)
            top = jnp.maximum(peak, jnp.max(scores, -1, keepdims=True))
            expo = jnp.exp(scores - top).astype(LOW)
            values = jnp.concatenate([only_half(v_ref[place, :], half), ones], 1)
            return top, acc * jnp.exp(peak - top) + matmul(expo, values)

        carry = (
            jnp.full((block, 1), -1e30, jnp.float32),
            jnp.zeros((block, 2 * width), jnp.float32),
        )
        carry = lax.fori_loop(0, here, partial(step, masked=False), carry)
        peak, acc = step(here, carry, True)
        summed = acc[:, width:]
        total += acc[:, :width] / summed
        logs = peak + jnp.log(summed)
        lse_ref[0, half : half + 1, :] = jnp.transpose(logs)[0:1, :]
    o_ref[...] = total.astype(o_ref.dtype)


def attend(packed, block):
    length, width = packed.shape[0], packed.shape[1] // 3
    pairs = width // 128
    return pl.pallas_call(
        partial(attend_kernel, block),
        grid=(pairs, length // block),
        in_specs=[
            pl.BlockSpec((block, 128), lambda pair, i: (i, pair)),
            pl.BlockSpec((length, 128), lambda pair, i: (0, pairs + pair)),
            pl.BlockSpec((length, 128), lambda pair, i: (0, 2 * pairs + pair)),
        ],
        out_specs=(
            pl.BlockSpec((block, 128), lambda pair, i: (i, pair)),
            pl.BlockSpec((1, 8, block), lambda pair, i: (pair, 0, i)),
        ),
        out_shape=(
            jax.ShapeDtypeStruct((length, width), LOW),
            jax.ShapeDtypeStruct((pairs, 8, length), jnp.float32),
        ),
        compiler_params=pltpu.CompilerParams(vmem_limit_bytes=VMEM_MOST),
        name="attend_forward",
    )(packed, packed, packed)


def attend_back_kernel(
    block, scale, q_ref, k_ref, v_ref, o_ref, g_ref, lse_ref, dq_ref, dk_ref, dv_ref, sum_ref, delta_ref
):
    here = pl.program_id(1)
    blocks = pl.num_programs(1)
    length = q_ref.shape[0]

    @pl.when(here == 0)
    def _():
        sum_ref[...] = jnp.zeros_like(sum_ref)

        @pl.loop(0, length // block)
        def _(index):
            place = pl.ds(pl.multiple_of(index * block, block), block)
            product = o_ref[place, :].astype(jnp.float32) * g_ref[place, :].astype(jnp.float32)
            row = lax.broadcasted_iota(jnp.int32, (8, product.shape[1]), 0)
            lane = lax.broadcasted_iota(jnp.int32, (8, product.shape[1]), 1)
            chooser = (row == lane // HEAD_DIM).astype(jnp.float32)
            delta_ref[:, place] = dot_dims(chooser, product, 1, 1, HIGHEST)

    keys, values = k_ref[...], v_ref[...]
    key_halves = [only_half(keys, half) for half in range(2)]
    value_halves = [only_half(values, half) for half in range(2)]
    rows = lax.broadcasted_iota(jnp.int32, (block, block), 0)
    cols = lax.broadcasted_iota(jnp.int32, (block, block), 1)

    def step(index, carry, masked):
        grad_keys, grad_values = carry
        place = pl.ds(pl.multiple_of(index * block, block), block)
        queries, grads = q_ref[place, :], g_ref[place, :]
        grad_queries = jnp.zeros((block, queries.shape[1]), jnp.float32)
        for half in range(2):
            scores = dot_dims(key_halves[half], queries, 1, 1)
            probs = jnp.exp(scores - lse_ref[0, half : half + 1, place])
            if masked:
                probs = jnp.where(rows <= cols, probs, 0.0)
            grad_probs = dot_dims(value_halves[half], grads, 1, 1)
            grad_scores = (probs * (grad_probs - delta_ref[half : half + 1, place])).astype(LOW)
            grad_values += matmul(probs.astype(LOW), only_half(grads, half))
            grad_keys += matmul(grad_scores, only_half(queries, half))
            grad_queries += dot_dims(grad_scores, key_halves[half], 0, 0)
        sum_ref[place, :] += grad_queries
        return grad_keys, grad_values

    zeros = jnp.zeros(keys.shape, jnp.float32)
    carry = step(here, (zeros, zeros), True)
    grad_keys, grad_values = lax.fori_loop(here + 1, blocks, partial(step, masked=False), carry)
    dk_ref[...] = grad_keys.astype(dk_ref.dtype)
    dv_ref[...] = grad_values.astype(dv_ref.dtype)

    @pl.when(here == blocks - 1)
    def _():
        dq_ref[...] = (sum_ref[...] * scale).astype(dq_ref.dtype)


def attend_back(packed, mixed, grads, lse, block, scale):
    length, width = packed.shape[0], packed.shape[1] // 3
    pairs = width // 128
    whole = pl.BlockSpec((length, 128), lambda pair, j: (0, pair))
    return pl.pallas_call(
        partial(attend_back_kernel, block, scale),
        grid=(pairs, length // block),
        in_specs=[
            whole,
            pl.BlockSpec((block, 128), lambda pair, j: (j, pairs + pair)),
            pl.BlockSpec((block, 128), lambda pair, j: (j, 2 * pairs + pair)),
            whole,
            whole,
            pl.BlockSpec((1, 8, length), lambda pair, j: (pair, 0, 0)),
        ],
        out_specs=(
            whole,
            pl.BlockSpec((block, 128), lambda pair, j: (j, pair)),
            pl.BlockSpec((block, 128), lambda pair, j: (j, pair)),
        ),
        out_shape=(jax.ShapeDtypeStruct((length, width), LOW),) * 3,
        scratch_shapes=[
            pltpu.VMEM((length, 128), jnp.float32),
            pltpu.VMEM((8, length), jnp.float32),
        ],
        compiler_params=pltpu.CompilerParams(vmem_limit_bytes=VMEM_MOST),
        name="attend_backward",
    )(packed, packed, packed, mixed, grads, lse)


def norm_factor(values):
    return lax.rsqrt(jnp.mean(values * values, -1, keepdims=True) + EPSILON)


def norm_back(values, gain, grads, factor):
    scaled = gain * grads
    shared = jnp.mean(values * scaled, -1, keepdims=True)
    return (
        factor * scaled - values * factor**3 * shared,
        jnp.sum(grads * values * factor, 0),
    )


def select(chooser, values):
    high = values.astype(LOW)
    rest = (values - high.astype(jnp.float32)).astype(LOW)
    return matmul(chooser, high) + matmul(chooser, rest)


def own_heads(weights, rank, team, padded):
    width, total = weights.shape
    count = HEADS // team * HEAD_DIM
    thirds = weights.reshape(width, total // (team * count), team * count)
    mine = lax.dynamic_slice_in_dim(thirds, rank * count, count, 2)
    mine = jnp.pad(mine, ((0, 0), (0, 0), (0, padded - count)))
    return mine.reshape(width, -1)


def body(
    inputs,
    cotangent,
    w_qkv,
    w_out,
    w_up,
    w_down,
    router_weight,
    gain_attn,
    gain_mlp,
    sel_idx,
    sel_count,
):
    seqs, tok_rows, width = inputs.shape
    narrow_size, wide_size = lax.axis_size("narrow"), lax.axis_size("wide")
    place = Place(narrow_size, seqs).locate()
    team, rank = place.team, place.rank
    length = narrow_size * tok_rows
    hidden_all = w_up.shape[1]
    paired = team == place.span
    count = HEADS // team * HEAD_DIM
    padded = -(-count // 128) * 128
    scale = HEAD_DIM ** (-0.5)
    entries = sel_idx.shape[1]
    block = min(512, length)

    lists = jnp.zeros((8, entries + 128), jnp.int32)
    lists = lists.at[:seqs, :entries].set(sel_idx).at[:seqs, entries].set(sel_count)
    factor = norm_factor(inputs)
    normed_in = (inputs * factor * gain_attn).astype(LOW)
    factors = jnp.broadcast_to(factor.reshape(seqs, 1, tok_rows), (seqs, 8, tok_rows))
    normed_low, cot_all, factors_all, lists_all = spread(
        Place(narrow_size, seqs), normed_in, cotangent, factors, lists, 1
    )
    mine = lists_all[place.seq // seqs, lax.rem(place.seq, seqs)]
    positions, amount = mine[:entries], mine[entries]

    w_own = own_heads(w_qkv, rank, team, padded)
    factor_all = factors_all[:, 0].reshape(length, 1)
    values = normed_low.astype(jnp.float32) / (factor_all * gain_attn)
    packed = matmul(normed_low, w_own)
    packed = jnp.concatenate([packed[:, :padded] * scale, packed[:, padded:]], 1).astype(LOW)
    mixed_own, lse = attend(packed, block)
    mixed_all = share(Place(narrow_size, seqs), mixed_own, 2)
    mixed_wide = jnp.concatenate([mixed_all[index] for index in range(team)], 1)
    w_out_pad = jnp.pad(w_out.reshape(team, count, width), ((0, 0), (0, padded - count), (0, 0)))
    w_out_pad = w_out_pad.reshape(team * padded, width)
    projected = matmul(mixed_wide, w_out_pad)
    resid = values + projected

    live = jnp.arange(entries, dtype=jnp.int32) < amount
    spots = jnp.where(live, positions, -1)
    chooser = (spots[:, None] == jnp.arange(length, dtype=jnp.int32)[None, :]).astype(LOW)
    picked = select(chooser, resid)
    router_sel = jnp.sum(picked * router_weight, -1, keepdims=True)
    rows_low = (picked * norm_factor(picked) * gain_mlp).astype(LOW)
    share_hidden = hidden_all // team
    if paired:
        unit = hidden_all // wide_size
        up_own = lax.dynamic_index_in_dim(
            w_up.reshape(width, wide_size // team, team, unit), rank, 2, False
        ).reshape(width, share_hidden)
        down_own = lax.dynamic_index_in_dim(
            w_down.reshape(wide_size // team, team, unit, width), rank, 1, False
        ).reshape(share_hidden, width)
    else:
        up_own = lax.dynamic_slice_in_dim(w_up, rank * share_hidden, share_hidden, 1)
        down_own = lax.dynamic_slice_in_dim(w_down, rank * share_hidden, share_hidden, 0)
    upper = matmul(rows_low, up_own)
    hidden, gelu_pull = jax.vjp(partial(jax.nn.gelu, approximate=False), upper)
    hidden = hidden.astype(LOW)
    branch_parts = share(Place(narrow_size, seqs), matmul(hidden, down_own).astype(LOW), 3)
    branch = jnp.sum(branch_parts.astype(jnp.float32), 0).astype(LOW).astype(jnp.float32)
    cot_sel = matmul(chooser, cot_all)
    grad_router = jnp.sum(cot_sel * branch, -1, keepdims=True)
    grad_branch = (router_sel * cot_sel).astype(LOW)
    grad_down = dot_dims(hidden, grad_branch, 0, 0)
    grad_upper = gelu_pull(dot_dims(grad_branch, down_own, 1, 1))[0].astype(LOW)
    grad_up = dot_dims(rows_low, grad_upper, 0, 0)
    grad_parts = share(Place(narrow_size, seqs), dot_dims(grad_upper, up_own, 1, 1).astype(LOW), 4)
    grad_rows = jnp.sum(grad_parts.astype(jnp.float32), 0).astype(LOW).astype(jnp.float32)
    grad_picked, grad_gain_mlp = norm_back(picked, gain_mlp, grad_rows, norm_factor(picked))
    grad_router_weight = jnp.sum(grad_router * picked, 0)
    extra = grad_picked + grad_router * router_weight
    cot_wide = cot_all.astype(jnp.float32)
    added = dot_dims(
        chooser,
        jnp.concatenate([(router_sel * branch).astype(LOW), extra.astype(LOW)], 1),
        0,
        0,
    )
    delta = (projected + added[:, :width]).astype(LOW)
    grad_resid = cot_wide + added[:, width:]
    grad_resid_low = grad_resid.astype(LOW)

    share_cols = width // team
    resid_cols = lax.dynamic_slice_in_dim(grad_resid_low, rank * share_cols, share_cols, 1)
    grad_out = dot_dims(mixed_wide, resid_cols, 0, 0)
    out_own = lax.dynamic_slice_in_dim(w_out_pad, rank * padded, padded, 0)
    grad_mixed = dot_dims(grad_resid_low, out_own, 1, 1).astype(LOW)
    grad_packed = jnp.concatenate(
        attend_back(packed, mixed_own, grad_mixed, lse, block, scale), 1
    )
    grad_qkv = dot_dims(normed_low, grad_packed, 0, 0)
    terms = split(Place(narrow_size, seqs), dot_dims(grad_packed, w_own, 1, 1).astype(LOW), 5)
    grad_normed = jnp.sum(terms.astype(jnp.float32), 0)
    share_rows = length // team

    def own_rows(array):
        return lax.dynamic_slice_in_dim(array, rank * share_rows, share_rows, 0)

    grad_norm, grad_gain_attn = norm_back(
        own_rows(values), gain_attn, grad_normed, own_rows(factor_all)
    )
    grad_rows_in = (own_rows(grad_resid) + grad_norm).astype(LOW)
    delta_back, grad_back = give_back(
        Place(narrow_size, seqs), [own_rows(delta), grad_rows_in], 6
    )
    output = inputs + delta_back.astype(jnp.float32)
    grad_inputs = grad_back.astype(jnp.float32)

    def thirds(array):
        return array.reshape(array.shape[0], 3, padded)[:, :, :count]

    grad_out = grad_out.reshape(team, padded, share_cols)[:, :count].reshape(-1, share_cols)
    if paired:
        chips = wide_size // team
        groups = [[chip * team + index for chip in range(chips)] for index in range(team)]

        def add_up(array):
            summed = lax.psum_scatter(
                array.astype(LOW), "wide", scatter_dimension=0, axis_index_groups=groups, tiled=True
            )
            return lax.psum(summed, "narrow")

        columns = jnp.concatenate([thirds(grad_qkv).reshape(width, -1), grad_up, grad_out], 1)
        columns = add_up(columns)
        sum_down = add_up(grad_down).astype(jnp.float32)
        pairs = [[chip * team + index for index in range(team)] for chip in range(chips)]
        columns = lax.all_to_all(
            columns.reshape(team, -1, columns.shape[1]),
            "wide",
            split_axis=0,
            concat_axis=0,
            axis_index_groups=pairs,
        ).astype(jnp.float32)
        rows_out = columns.shape[1]
        first, second = 3 * count, 3 * count + share_hidden
        sum_qkv = columns[:, :, :first].reshape(team, rows_out, 3, count)
        sum_qkv = sum_qkv.transpose(1, 2, 0, 3).reshape(rows_out, -1)
        sum_up = columns[:, :, first:second].reshape(team, rows_out, chips, unit)
        sum_up = sum_up.transpose(1, 2, 0, 3).reshape(rows_out, -1)
        sum_out = columns[:, :, second:].transpose(1, 0, 2).reshape(rows_out, -1)
    else:

        def add_up(array):
            summed = lax.psum_scatter(
                array.astype(LOW), "wide", scatter_dimension=0, tiled=True
            )
            return lax.psum(summed, "narrow").astype(jnp.float32)

        def spot(shape, part, start):
            return lax.dynamic_update_slice(jnp.zeros(shape, jnp.float32), part, start)

        sum_qkv = spot((width, 3, team * count), thirds(grad_qkv), (0, 0, rank * count))
        sum_qkv = add_up(sum_qkv.reshape(width, -1))
        sum_out = add_up(spot(w_out.shape, grad_out, (0, rank * share_cols)))
        sum_up = add_up(spot(w_up.shape, grad_up, (0, rank * share_hidden)))
        sum_down = add_up(spot(w_down.shape, grad_down, (rank * share_hidden, 0)))

    first_rank = (rank == 0).astype(jnp.float32)
    small = lax.psum(
        jnp.stack([grad_router_weight * first_rank, grad_gain_attn, grad_gain_mlp * first_rank]),
        ("wide", "narrow"),
    )
    return (
        output,
        grad_inputs,
        sum_qkv,
        sum_out,
        sum_up,
        sum_down,
        small[0],
        small[1],
        small[2],
    )


def solution(mesh):
    in_specs = (
        P("wide", "narrow", None),
        P("wide", "narrow", None),
        P(),
        P(),
        P(),
        P(),
        P(),
        P(),
        P(),
        P("wide", None),
        P("wide"),
    )
    out_specs = (
        P("wide", "narrow", None),
        P("wide", "narrow", None),
        P("wide", None),
        P("wide", None),
        P("wide", None),
        P("wide", None),
        P(),
        P(),
        P(),
    )
    return jax.shard_map(body, mesh=mesh, in_specs=in_specs, out_specs=out_specs, check_vma=False)
```

```python
from functools import partial

import jax
import jax.numpy as jnp
from jax import lax
from jax.experimental import pallas as pl
from jax.experimental.pallas import tpu as pltpu
from jax.sharding import PartitionSpec as P

HEADS = 12
HEAD_DIM = 64
EPSILON = 1e-06
MESH = pl.DeviceIdType.MESH
LOW = jnp.bfloat16
HIGHEST = lax.Precision.HIGHEST
VMEM_MOST = 56 * 1024 * 1024


def matmul(left, right):
    return jnp.dot(left, right, preferred_element_type=jnp.float32)


def dot_dims(left, right, left_dim, right_dim, precision=None):
    return lax.dot_general(
        left,
        right,
        (((left_dim,), (right_dim,)), ((), ())),
        precision=precision,
        preferred_element_type=jnp.float32,
    )


class Place:
    def __init__(self, narrow_size, seqs):
        self.narrow_size = narrow_size
        self.span = max(1, 8 // narrow_size)
        self.seqs = seqs
        self.members = self.span * narrow_size
        self.team = self.members // (seqs * self.span)

    def locate(self):
        wide, narrow = lax.axis_index("wide"), lax.axis_index("narrow")
        self.narrow = narrow
        self.offset = lax.rem(wide, self.span)
        self.group = wide // self.span
        self.me = narrow * self.span + self.offset
        self.seq = self.me // self.team
        self.rank = lax.rem(self.me, self.team)
        return self

    def device(self, member):
        return {
            "wide": self.group * self.span + lax.rem(member, self.span),
            "narrow": member // self.span,
        }

    def sibling(self, step):
        return self.seq * self.team + lax.rem(self.rank + step, self.team)

    def greet_group(self):
        barrier = pltpu.get_barrier_semaphore()
        for step in range(1, self.members):
            other = lax.rem(self.me + step, self.members)
            pl.semaphore_signal(
                barrier, inc=1, device_id=self.device(other), device_id_type=MESH
            )
        pl.semaphore_wait(barrier, self.members - 1)

    def greet_team(self):
        barrier = pltpu.get_barrier_semaphore()
        for step in range(1, self.team):
            pl.semaphore_signal(
                barrier, inc=1, device_id=self.device(self.sibling(step)), device_id_type=MESH
            )
        pl.semaphore_wait(barrier, self.team - 1)


def remote(src, dst, send, recv, device):
    return pltpu.make_async_remote_copy(
        src_ref=src, dst_ref=dst, send_sem=send, recv_sem=recv, device_id=device, device_id_type=MESH
    )


def spread_start(place, src, dst, sems):
    send, recv, fsend, frecv, local = sems
    rows = src.shape[1]
    part = rows // place.team
    for seq in range(place.seqs):
        for rank in range(place.team):
            target = (place.seqs * place.offset + seq) * place.team + rank
            source_rows = src.at[seq, pl.ds(rank * part, part)]
            start = pl.multiple_of(place.narrow * rows + rank * part, part)
            landing = dst.at[pl.ds(start, part)]

            @pl.when(target == place.me)
            def _():
                pltpu.make_async_copy(source_rows, landing, local).start()

            @pl.when(target != place.me)
            def _():
                remote(
                    source_rows,
                    landing,
                    send.at[seq, rank],
                    recv.at[place.narrow],
                    place.device(target),
                ).start()


def spread_forward(place, src, dst, sems):
    send, recv, fsend, frecv, local = sems
    rows = src.shape[1]
    part = rows // place.team

    def landed(block, rank):
        return dst.at[pl.ds(pl.multiple_of(block * rows + rank * part, part), part)]

    for block in range(place.narrow_size):
        source = block * place.span + place.seq // place.seqs
        mine = landed(block, place.rank)

        @pl.when(source == place.me)
        def _():
            pltpu.make_async_copy(mine, mine, local).wait()

        @pl.when(source != place.me)
        def _():
            remote(
                mine, mine, send.at[0, 0], recv.at[block], place.device(place.sibling(1))
            ).wait_recv()

        for step in range(1, place.team):
            remote(
                mine,
                mine,
                fsend.at[block, step - 1],
                frecv.at[block, step - 1],
                place.device(place.sibling(step)),
            ).start()


def spread_finish(place, src, dst, sems):
    send, recv, fsend, frecv, local = sems
    rows = src.shape[1]
    part = rows // place.team

    def landed(block, rank):
        return dst.at[pl.ds(pl.multiple_of(block * rows + rank * part, part), part)]

    for block in range(place.narrow_size):
        for step in range(1, place.team):
            other = lax.rem(place.rank + place.team - step, place.team)
            theirs = landed(block, other)
            copy = remote(
                landed(block, place.rank),
                theirs,
                fsend.at[block, step - 1],
                frecv.at[block, step - 1],
                place.device(place.sibling(step)),
            )
            copy.wait_send()
            copy.wait_recv()
    for seq in range(place.seqs):
        for rank in range(place.team):
            target = (place.seqs * place.offset + seq) * place.team + rank

            @pl.when(target != place.me)
            def _():
                source_rows = src.at[seq, pl.ds(rank * part, part)]
                remote(
                    source_rows,
                    source_rows,
                    send.at[seq, rank],
                    recv.at[0],
                    place.device(target),
                ).wait_send()


def spread_sems(place):
    return [
        pltpu.SemaphoreType.DMA((place.seqs, place.team)),
        pltpu.SemaphoreType.DMA((place.narrow_size,)),
        pltpu.SemaphoreType.DMA((place.narrow_size, place.team - 1)),
        pltpu.SemaphoreType.DMA((place.narrow_size, place.team - 1)),
        pltpu.SemaphoreType.DMA(()),
    ]


def spread_kernel(place, x_ref, f_ref, l_ref, xs_ref, fs_ref, ls_ref, *sems):
    lsend, lrecv, llocal, rsend, rrecv, rlocal = sems[:6]
    sems = sems[6:]
    place.locate()
    place.greet_group()
    own = ls_ref.at[place.offset]
    pltpu.make_async_copy(l_ref, own, llocal).start()
    for step in range(1, place.span):
        other = place.narrow * place.span + lax.rem(place.offset + step, place.span)
        remote(l_ref, own, lsend.at[step - 1], lrecv.at[step - 1], place.device(other)).start()

    def factors(act_local, act_remote):
        for seq in range(place.seqs):
            for rank in range(place.team):
                target = (place.seqs * place.offset + seq) * place.team + rank

                @pl.when(target == place.me)
                def _():
                    act_local(
                        pltpu.make_async_copy(f_ref.at[seq], fs_ref.at[place.narrow], rlocal)
                    )

                @pl.when(target != place.me)
                def _():
                    act_remote(
                        remote(
                            f_ref.at[seq],
                            fs_ref.at[place.narrow],
                            rsend.at[seq, rank],
                            rrecv.at[place.narrow],
                            place.device(target),
                        )
                    )

    factors(lambda copy: copy.start(), lambda copy: copy.start())
    spread_start(place, x_ref, xs_ref, sems)
    for step in range(1, place.span):
        back = lax.rem(place.offset + place.span - step, place.span)
        other = place.narrow * place.span + lax.rem(place.offset + step, place.span)
        copy = remote(
            l_ref, ls_ref.at[back], lsend.at[step - 1], lrecv.at[step - 1], place.device(other)
        )
        copy.wait_send()
        copy.wait_recv()
    pltpu.make_async_copy(l_ref, own, llocal).wait()
    factors(lambda copy: copy.wait(), lambda copy: copy.wait_send())
    for block in range(place.narrow_size):
        source = block * place.span + place.seq // place.seqs

        @pl.when(source != place.me)
        def _():
            remote(
                f_ref.at[0],
                fs_ref.at[block],
                rsend.at[0, 0],
                rrecv.at[block],
                place.device(place.sibling(1)),
            ).wait_recv()

    spread_forward(place, x_ref, xs_ref, sems)
    spread_finish(place, x_ref, xs_ref, sems)


def spread(place, rows_low, factors, lists, collective_id):
    seqs, rows, width = rows_low.shape
    full = jax.ShapeDtypeStruct((place.narrow_size * rows, width), LOW)
    anywhere = pl.BlockSpec(memory_space=pl.ANY)
    inside = pl.BlockSpec(memory_space=pltpu.VMEM)
    steps = max(1, place.span - 1)
    return pl.pallas_call(
        partial(spread_kernel, place),
        out_shape=(
            full,
            jax.ShapeDtypeStruct((place.narrow_size,) + factors.shape[1:], factors.dtype),
            jax.ShapeDtypeStruct((place.span,) + lists.shape, lists.dtype),
        ),
        in_specs=[inside] * 3,
        out_specs=(anywhere,) * 3,
        scratch_shapes=[
            pltpu.SemaphoreType.DMA((steps,)),
            pltpu.SemaphoreType.DMA((steps,)),
            pltpu.SemaphoreType.DMA(()),
            pltpu.SemaphoreType.DMA((place.seqs, place.team)),
            pltpu.SemaphoreType.DMA((place.narrow_size,)),
            pltpu.SemaphoreType.DMA(()),
        ]
        + spread_sems(place),
        compiler_params=pltpu.CompilerParams(
            collective_id=collective_id, has_side_effects=True, vmem_limit_bytes=VMEM_MOST
        ),
        name="spread_rows",
    )(rows_low, factors, lists)


def share_kernel(place, x_ref, out_ref, send, recv, local):
    place.locate()
    place.greet_team()
    own = out_ref.at[place.rank]
    pltpu.make_async_copy(x_ref, own, local).start()
    for step in range(1, place.team):
        remote(
            x_ref, own, send.at[step - 1], recv.at[step - 1], place.device(place.sibling(step))
        ).start()
    for step in range(1, place.team):
        back = lax.rem(place.rank + place.team - step, place.team)
        copy = remote(
            x_ref,
            out_ref.at[back],
            send.at[step - 1],
            recv.at[step - 1],
            place.device(place.sibling(step)),
        )
        copy.wait_send()
        copy.wait_recv()
    pltpu.make_async_copy(x_ref, own, local).wait()


def share(place, part, collective_id):
    anywhere = pl.BlockSpec(memory_space=pl.ANY)
    return pl.pallas_call(
        partial(share_kernel, place),
        out_shape=jax.ShapeDtypeStruct((place.team,) + part.shape, part.dtype),
        in_specs=[pl.BlockSpec(memory_space=pltpu.VMEM)],
        out_specs=anywhere,
        scratch_shapes=[
            pltpu.SemaphoreType.DMA((place.team - 1,)),
            pltpu.SemaphoreType.DMA((place.team - 1,)),
            pltpu.SemaphoreType.DMA(()),
        ],
        compiler_params=pltpu.CompilerParams(
            collective_id=collective_id, has_side_effects=True, vmem_limit_bytes=VMEM_MOST
        ),
        name="share_parts",
    )(part)


def split_kernel(place, x_ref, out_ref, send, recv, local):
    place.locate()
    place.greet_team()
    rows = x_ref.shape[0] // place.team

    def rows_of(rank):
        return x_ref.at[pl.ds(pl.multiple_of(rank * rows, rows), rows)]

    pltpu.make_async_copy(rows_of(place.rank), out_ref.at[0], local).start()
    for step in range(1, place.team):
        target = lax.rem(place.rank + step, place.team)
        remote(
            rows_of(target),
            out_ref.at[step],
            send.at[step - 1],
            recv.at[step - 1],
            place.device(place.sibling(step)),
        ).start()
    for step in range(1, place.team):
        target = lax.rem(place.rank + step, place.team)
        copy = remote(
            rows_of(target),
            out_ref.at[step],
            send.at[step - 1],
            recv.at[step - 1],
            place.device(place.sibling(step)),
        )
        copy.wait_send()
        copy.wait_recv()
    pltpu.make_async_copy(rows_of(place.rank), out_ref.at[0], local).wait()


def split(place, terms, collective_id):
    anywhere = pl.BlockSpec(memory_space=pl.ANY)
    rows, width = terms.shape
    return pl.pallas_call(
        partial(split_kernel, place),
        out_shape=jax.ShapeDtypeStruct((place.team, rows // place.team, width), terms.dtype),
        in_specs=[pl.BlockSpec(memory_space=pltpu.VMEM)],
        out_specs=anywhere,
        scratch_shapes=[
            pltpu.SemaphoreType.DMA((place.team - 1,)),
            pltpu.SemaphoreType.DMA((place.team - 1,)),
            pltpu.SemaphoreType.DMA(()),
        ],
        compiler_params=pltpu.CompilerParams(
            collective_id=collective_id, has_side_effects=True, vmem_limit_bytes=VMEM_MOST
        ),
        name="split_terms",
    )(terms)


def give_back_kernel(place, *refs):
    count = (len(refs) - 3) // 2
    sources, results = refs[:count], refs[count : 2 * count]
    send, recv, local = refs[2 * count :]
    place.locate()
    place.greet_group()
    rows = results[0].shape[1]
    blocks = place.narrow_size // place.team

    def each(act):
        for item, (src, dst) in enumerate(zip(sources, results)):
            for index in range(blocks):
                block = place.rank * blocks + index
                target = block * place.span + place.seq // place.seqs
                seq = lax.rem(place.seq, place.seqs)
                act(item, index, src.at[pl.ds(index * rows, rows)], dst.at[seq], seq, target)

    def begin(item, index, rows_here, landing, seq, target):
        @pl.when(target == place.me)
        def _():
            pltpu.make_async_copy(rows_here, landing, local.at[item, index]).start()

        @pl.when(target != place.me)
        def _():
            remote(
                rows_here,
                landing,
                send.at[item, index],
                recv.at[item, seq],
                place.device(target),
            ).start()

    def end(item, index, rows_here, landing, seq, target):
        @pl.when(target == place.me)
        def _():
            pltpu.make_async_copy(rows_here, landing, local.at[item, index]).wait()

        @pl.when(target != place.me)
        def _():
            remote(
                rows_here,
                landing,
                send.at[item, index],
                recv.at[item, seq],
                place.device(target),
            ).wait_send()

    each(begin)
    for item, dst in enumerate(results):
        for seq in range(place.seqs):
            source = (place.seqs * place.offset + seq) * place.team + place.narrow // blocks

            @pl.when(source != place.me)
            def _():
                remote(
                    dst.at[seq],
                    dst.at[seq],
                    send.at[0, 0],
                    recv.at[item, seq],
                    place.device(source),
                ).wait_recv()

    each(end)


def give_back(place, arrays, collective_id):
    anywhere = pl.BlockSpec(memory_space=pl.ANY)
    blocks = place.narrow_size // place.team
    rows, width = arrays[0].shape
    count = len(arrays)
    return pl.pallas_call(
        partial(give_back_kernel, place),
        out_shape=tuple(
            jax.ShapeDtypeStruct((place.seqs, rows // blocks, width), a.dtype) for a in arrays
        ),
        in_specs=[pl.BlockSpec(memory_space=pltpu.VMEM)] * count,
        out_specs=(anywhere,) * count,
        scratch_shapes=[
            pltpu.SemaphoreType.DMA((count, blocks)),
            pltpu.SemaphoreType.DMA((count, place.seqs)),
            pltpu.SemaphoreType.DMA((count, blocks)),
        ],
        compiler_params=pltpu.CompilerParams(
            collective_id=collective_id, has_side_effects=True, vmem_limit_bytes=VMEM_MOST
        ),
        name="give_back_rows",
    )(*arrays)


def half_lanes(half, shape):
    lane = lax.broadcasted_iota(jnp.int32, shape, len(shape) - 1)
    return (lane // HEAD_DIM) == half


def only_half(values, half):
    return jnp.where(half_lanes(half, values.shape), values, jnp.zeros_like(values))


def attend_kernel(place, block, q_ref, k_ref, v_ref, c_ref, o_ref, lse_ref, cs_ref, *sems):
    place.locate()
    now, here = pl.program_id(0), pl.program_id(1)

    @pl.when((now == 0) & (here == 0))
    def _():
        place.greet_group()
        spread_start(place, c_ref, cs_ref, sems)

    @pl.when((now == pl.num_programs(0) - 1) & (here == 0))
    def _():
        spread_forward(place, c_ref, cs_ref, sems)

    attend_block(block, here, q_ref, k_ref, v_ref, o_ref, lse_ref)

    @pl.when((now == pl.num_programs(0) - 1) & (here == pl.num_programs(1) - 1))
    def _():
        spread_finish(place, c_ref, cs_ref, sems)


def attend_block(block, here, q_ref, k_ref, v_ref, o_ref, lse_ref):
    pair = q_ref[...]
    width = pair.shape[1]
    ones = jnp.ones((block, width), LOW)
    rows = lax.broadcasted_iota(jnp.int32, (block, block), 0)
    cols = lax.broadcasted_iota(jnp.int32, (block, block), 1)
    total = jnp.zeros((block, width), jnp.float32)
    for half in range(2):
        query = only_half(pair, half)

        def step(index, carry, masked):
            peak, acc = carry
            place = pl.ds(pl.multiple_of(index * block, block), block)
            scores = dot_dims(query, k_ref[place, :], 1, 1)
            if masked:
                scores = jnp.where(cols <= rows, scores, -1e30)
            top = jnp.maximum(peak, jnp.max(scores, -1, keepdims=True))
            expo = jnp.exp(scores - top).astype(LOW)
            values = jnp.concatenate([only_half(v_ref[place, :], half), ones], 1)
            return top, acc * jnp.exp(peak - top) + matmul(expo, values)

        carry = (
            jnp.full((block, 1), -1e30, jnp.float32),
            jnp.zeros((block, 2 * width), jnp.float32),
        )
        carry = lax.fori_loop(0, here, partial(step, masked=False), carry)
        peak, acc = step(here, carry, True)
        summed = acc[:, width:]
        total += acc[:, :width] / summed
        logs = peak + jnp.log(summed)
        lse_ref[0, half : half + 1, :] = jnp.transpose(logs)[0:1, :]
    o_ref[...] = total.astype(o_ref.dtype)


def attend(place, packed, cotangent, block, collective_id):
    length, width = packed.shape[0], packed.shape[1] // 3
    pairs = width // 128
    return pl.pallas_call(
        partial(attend_kernel, place, block),
        grid=(pairs, length // block),
        in_specs=[
            pl.BlockSpec((block, 128), lambda pair, i: (i, pair)),
            pl.BlockSpec((length, 128), lambda pair, i: (0, pairs + pair)),
            pl.BlockSpec((length, 128), lambda pair, i: (0, 2 * pairs + pair)),
            pl.BlockSpec(memory_space=pl.ANY),
        ],
        out_specs=(
            pl.BlockSpec((block, 128), lambda pair, i: (i, pair)),
            pl.BlockSpec((1, 8, block), lambda pair, i: (pair, 0, i)),
            pl.BlockSpec(memory_space=pl.ANY),
        ),
        out_shape=(
            jax.ShapeDtypeStruct((length, width), LOW),
            jax.ShapeDtypeStruct((pairs, 8, length), jnp.float32),
            jax.ShapeDtypeStruct((length, cotangent.shape[2]), LOW),
        ),
        scratch_shapes=spread_sems(place),
        compiler_params=pltpu.CompilerParams(
            collective_id=collective_id, has_side_effects=True, vmem_limit_bytes=VMEM_MOST
        ),
        name="attend_forward",
    )(packed, packed, packed, cotangent)


def attend_back_kernel(
    block, scale, q_ref, k_ref, v_ref, o_ref, g_ref, lse_ref, dq_ref, dk_ref, dv_ref, sum_ref, delta_ref
):
    here = pl.program_id(1)
    blocks = pl.num_programs(1)
    length = q_ref.shape[0]

    @pl.when(here == 0)
    def _():
        sum_ref[...] = jnp.zeros_like(sum_ref)

        @pl.loop(0, length // block)
        def _(index):
            place = pl.ds(pl.multiple_of(index * block, block), block)
            product = o_ref[place, :].astype(jnp.float32) * g_ref[place, :].astype(jnp.float32)
            row = lax.broadcasted_iota(jnp.int32, (8, product.shape[1]), 0)
            lane = lax.broadcasted_iota(jnp.int32, (8, product.shape[1]), 1)
            chooser = (row == lane // HEAD_DIM).astype(jnp.float32)
            delta_ref[:, place] = dot_dims(chooser, product, 1, 1, HIGHEST)

    keys, values = k_ref[...], v_ref[...]
    key_halves = [only_half(keys, half) for half in range(2)]
    value_halves = [only_half(values, half) for half in range(2)]
    rows = lax.broadcasted_iota(jnp.int32, (block, block), 0)
    cols = lax.broadcasted_iota(jnp.int32, (block, block), 1)

    def step(index, carry, masked):
        grad_keys, grad_values = carry
        place = pl.ds(pl.multiple_of(index * block, block), block)
        queries, grads = q_ref[place, :], g_ref[place, :]
        grad_queries = jnp.zeros((block, queries.shape[1]), jnp.float32)
        for half in range(2):
            scores = dot_dims(key_halves[half], queries, 1, 1)
            probs = jnp.exp(scores - lse_ref[0, half : half + 1, place])
            if masked:
                probs = jnp.where(rows <= cols, probs, 0.0)
            grad_probs = dot_dims(value_halves[half], grads, 1, 1)
            grad_scores = (probs * (grad_probs - delta_ref[half : half + 1, place])).astype(LOW)
            grad_values += matmul(probs.astype(LOW), only_half(grads, half))
            grad_keys += matmul(grad_scores, only_half(queries, half))
            grad_queries += dot_dims(grad_scores, key_halves[half], 0, 0)
        sum_ref[place, :] += grad_queries
        return grad_keys, grad_values

    zeros = jnp.zeros(keys.shape, jnp.float32)
    carry = step(here, (zeros, zeros), True)
    grad_keys, grad_values = lax.fori_loop(here + 1, blocks, partial(step, masked=False), carry)
    dk_ref[...] = grad_keys.astype(dk_ref.dtype)
    dv_ref[...] = grad_values.astype(dv_ref.dtype)

    @pl.when(here == blocks - 1)
    def _():
        dq_ref[...] = (sum_ref[...] * scale).astype(dq_ref.dtype)


def attend_back(packed, mixed, grads, lse, block, scale):
    length, width = packed.shape[0], packed.shape[1] // 3
    pairs = width // 128
    whole = pl.BlockSpec((length, 128), lambda pair, j: (0, pair))
    return pl.pallas_call(
        partial(attend_back_kernel, block, scale),
        grid=(pairs, length // block),
        in_specs=[
            whole,
            pl.BlockSpec((block, 128), lambda pair, j: (j, pairs + pair)),
            pl.BlockSpec((block, 128), lambda pair, j: (j, 2 * pairs + pair)),
            whole,
            whole,
            pl.BlockSpec((1, 8, length), lambda pair, j: (pair, 0, 0)),
        ],
        out_specs=(
            whole,
            pl.BlockSpec((block, 128), lambda pair, j: (j, pair)),
            pl.BlockSpec((block, 128), lambda pair, j: (j, pair)),
        ),
        out_shape=(jax.ShapeDtypeStruct((length, width), LOW),) * 3,
        scratch_shapes=[
            pltpu.VMEM((length, 128), jnp.float32),
            pltpu.VMEM((8, length), jnp.float32),
        ],
        compiler_params=pltpu.CompilerParams(vmem_limit_bytes=VMEM_MOST),
        name="attend_backward",
    )(packed, packed, packed, mixed, grads, lse)


def norm_factor(values):
    return lax.rsqrt(jnp.mean(values * values, -1, keepdims=True) + EPSILON)


def norm_back(values, gain, grads, factor):
    scaled = gain * grads
    shared = jnp.mean(values * scaled, -1, keepdims=True)
    return (
        factor * scaled - values * factor**3 * shared,
        jnp.sum(grads * values * factor, 0),
    )


def select(chooser, values):
    high = values.astype(LOW)
    rest = (values - high.astype(jnp.float32)).astype(LOW)
    return matmul(chooser, high) + matmul(chooser, rest)


def own_heads(weights, rank, team, padded):
    width, total = weights.shape
    count = HEADS // team * HEAD_DIM
    thirds = weights.reshape(width, total // (team * count), team * count)
    mine = lax.dynamic_slice_in_dim(thirds, rank * count, count, 2)
    mine = jnp.pad(mine, ((0, 0), (0, 0), (0, padded - count)))
    return mine.reshape(width, -1)


def body(
    inputs,
    cotangent,
    w_qkv,
    w_out,
    w_up,
    w_down,
    router_weight,
    gain_attn,
    gain_mlp,
    sel_idx,
    sel_count,
):
    seqs, tok_rows, width = inputs.shape
    narrow_size, wide_size = lax.axis_size("narrow"), lax.axis_size("wide")
    place = Place(narrow_size, seqs).locate()
    team, rank = place.team, place.rank
    length = narrow_size * tok_rows
    hidden_all = w_up.shape[1]
    paired = team == place.span
    count = HEADS // team * HEAD_DIM
    padded = -(-count // 128) * 128
    scale = HEAD_DIM ** (-0.5)
    entries = sel_idx.shape[1]
    block = min(512, length)

    lists = jnp.zeros((8, entries + 128), jnp.int32)
    lists = lists.at[:seqs, :entries].set(sel_idx).at[:seqs, entries].set(sel_count)
    factor = norm_factor(inputs)
    normed_in = (inputs * factor * gain_attn).astype(LOW)
    factors = jnp.broadcast_to(factor.reshape(seqs, 1, tok_rows), (seqs, 8, tok_rows))
    normed_low, factors_all, lists_all = spread(
        Place(narrow_size, seqs), normed_in, factors, lists, 1
    )
    mine = lists_all[place.seq // seqs, lax.rem(place.seq, seqs)]
    positions, amount = mine[:entries], mine[entries]

    w_own = own_heads(w_qkv, rank, team, padded)
    factor_all = factors_all[:, 0].reshape(length, 1)
    values = normed_low.astype(jnp.float32) / (factor_all * gain_attn)
    packed = matmul(normed_low, w_own)
    packed = jnp.concatenate([packed[:, :padded] * scale, packed[:, padded:]], 1).astype(LOW)
    mixed_own, lse, cot_all = attend(Place(narrow_size, seqs), packed, cotangent, block, 7)
    mixed_all = share(Place(narrow_size, seqs), mixed_own, 2)
    mixed_wide = jnp.concatenate([mixed_all[index] for index in range(team)], 1)
    w_out_pad = jnp.pad(w_out.reshape(team, count, width), ((0, 0), (0, padded - count), (0, 0)))
    w_out_pad = w_out_pad.reshape(team * padded, width)
    projected = matmul(mixed_wide, w_out_pad)
    resid = values + projected

    live = jnp.arange(entries, dtype=jnp.int32) < amount
    spots = jnp.where(live, positions, -1)
    chooser = (spots[:, None] == jnp.arange(length, dtype=jnp.int32)[None, :]).astype(LOW)
    picked = select(chooser, resid)
    router_sel = jnp.sum(picked * router_weight, -1, keepdims=True)
    rows_low = (picked * norm_factor(picked) * gain_mlp).astype(LOW)
    share_hidden = hidden_all // team
    if paired:
        unit = hidden_all // wide_size
        up_own = lax.dynamic_index_in_dim(
            w_up.reshape(width, wide_size // team, team, unit), rank, 2, False
        ).reshape(width, share_hidden)
        down_own = lax.dynamic_index_in_dim(
            w_down.reshape(wide_size // team, team, unit, width), rank, 1, False
        ).reshape(share_hidden, width)
    else:
        up_own = lax.dynamic_slice_in_dim(w_up, rank * share_hidden, share_hidden, 1)
        down_own = lax.dynamic_slice_in_dim(w_down, rank * share_hidden, share_hidden, 0)
    upper = matmul(rows_low, up_own)
    hidden, gelu_pull = jax.vjp(partial(jax.nn.gelu, approximate=False), upper)
    hidden = hidden.astype(LOW)
    branch_parts = share(Place(narrow_size, seqs), matmul(hidden, down_own).astype(LOW), 3)
    branch = jnp.sum(branch_parts.astype(jnp.float32), 0).astype(LOW).astype(jnp.float32)
    cot_sel = matmul(chooser, cot_all)
    grad_router = jnp.sum(cot_sel * branch, -1, keepdims=True)
    grad_branch = (router_sel * cot_sel).astype(LOW)
    grad_down = dot_dims(hidden, grad_branch, 0, 0)
    grad_upper = gelu_pull(dot_dims(grad_branch, down_own, 1, 1))[0].astype(LOW)
    grad_up = dot_dims(rows_low, grad_upper, 0, 0)
    grad_parts = share(Place(narrow_size, seqs), dot_dims(grad_upper, up_own, 1, 1).astype(LOW), 4)
    grad_rows = jnp.sum(grad_parts.astype(jnp.float32), 0).astype(LOW).astype(jnp.float32)
    grad_picked, grad_gain_mlp = norm_back(picked, gain_mlp, grad_rows, norm_factor(picked))
    grad_router_weight = jnp.sum(grad_router * picked, 0)
    extra = grad_picked + grad_router * router_weight
    cot_wide = cot_all.astype(jnp.float32)
    added = dot_dims(
        chooser,
        jnp.concatenate([(router_sel * branch).astype(LOW), extra.astype(LOW)], 1),
        0,
        0,
    )
    delta = (projected + added[:, :width]).astype(LOW)
    grad_resid = cot_wide + added[:, width:]
    grad_resid_low = grad_resid.astype(LOW)

    share_cols = width // team
    resid_cols = lax.dynamic_slice_in_dim(grad_resid_low, rank * share_cols, share_cols, 1)
    grad_out = dot_dims(mixed_wide, resid_cols, 0, 0)
    out_own = lax.dynamic_slice_in_dim(w_out_pad, rank * padded, padded, 0)
    grad_mixed = dot_dims(grad_resid_low, out_own, 1, 1).astype(LOW)
    grad_packed = jnp.concatenate(
        attend_back(packed, mixed_own, grad_mixed, lse, block, scale), 1
    )
    grad_qkv = dot_dims(normed_low, grad_packed, 0, 0)
    terms = split(Place(narrow_size, seqs), dot_dims(grad_packed, w_own, 1, 1).astype(LOW), 5)
    grad_normed = jnp.sum(terms.astype(jnp.float32), 0)
    share_rows = length // team

    def own_rows(array):
        return lax.dynamic_slice_in_dim(array, rank * share_rows, share_rows, 0)

    grad_norm, grad_gain_attn = norm_back(
        own_rows(values), gain_attn, grad_normed, own_rows(factor_all)
    )
    grad_rows_in = (own_rows(grad_resid) + grad_norm).astype(LOW)
    delta_back, grad_back = give_back(
        Place(narrow_size, seqs), [own_rows(delta), grad_rows_in], 6
    )
    output = inputs + delta_back.astype(jnp.float32)
    grad_inputs = grad_back.astype(jnp.float32)

    def thirds(array):
        return array.reshape(array.shape[0], 3, padded)[:, :, :count]

    grad_out = grad_out.reshape(team, padded, share_cols)[:, :count].reshape(-1, share_cols)
    if paired:
        chips = wide_size // team
        groups = [[chip * team + index for chip in range(chips)] for index in range(team)]

        def add_up(array):
            summed = lax.psum_scatter(
                array.astype(LOW), "wide", scatter_dimension=0, axis_index_groups=groups, tiled=True
            )
            return lax.psum(summed, "narrow")

        columns = jnp.concatenate([thirds(grad_qkv).reshape(width, -1), grad_up, grad_out], 1)
        columns = add_up(columns)
        sum_down = add_up(grad_down).astype(jnp.float32)
        pairs = [[chip * team + index for index in range(team)] for chip in range(chips)]
        columns = lax.all_to_all(
            columns.reshape(team, -1, columns.shape[1]),
            "wide",
            split_axis=0,
            concat_axis=0,
            axis_index_groups=pairs,
        ).astype(jnp.float32)
        rows_out = columns.shape[1]
        first, second = 3 * count, 3 * count + share_hidden
        sum_qkv = columns[:, :, :first].reshape(team, rows_out, 3, count)
        sum_qkv = sum_qkv.transpose(1, 2, 0, 3).reshape(rows_out, -1)
        sum_up = columns[:, :, first:second].reshape(team, rows_out, chips, unit)
        sum_up = sum_up.transpose(1, 2, 0, 3).reshape(rows_out, -1)
        sum_out = columns[:, :, second:].transpose(1, 0, 2).reshape(rows_out, -1)
    else:

        def add_up(array):
            summed = lax.psum_scatter(
                array.astype(LOW), "wide", scatter_dimension=0, tiled=True
            )
            return lax.psum(summed, "narrow").astype(jnp.float32)

        def spot(shape, part, start):
            return lax.dynamic_update_slice(jnp.zeros(shape, jnp.float32), part, start)

        sum_qkv = spot((width, 3, team * count), thirds(grad_qkv), (0, 0, rank * count))
        sum_qkv = add_up(sum_qkv.reshape(width, -1))
        sum_out = add_up(spot(w_out.shape, grad_out, (0, rank * share_cols)))
        sum_up = add_up(spot(w_up.shape, grad_up, (0, rank * share_hidden)))
        sum_down = add_up(spot(w_down.shape, grad_down, (rank * share_hidden, 0)))

    first_rank = (rank == 0).astype(jnp.float32)
    small = lax.psum(
        jnp.stack([grad_router_weight * first_rank, grad_gain_attn, grad_gain_mlp * first_rank]),
        ("wide", "narrow"),
    )
    return (
        output,
        grad_inputs,
        sum_qkv,
        sum_out,
        sum_up,
        sum_down,
        small[0],
        small[1],
        small[2],
    )


def solution(mesh):
    in_specs = (
        P("wide", "narrow", None),
        P("wide", "narrow", None),
        P(),
        P(),
        P(),
        P(),
        P(),
        P(),
        P(),
        P("wide", None),
        P("wide"),
    )
    out_specs = (
        P("wide", "narrow", None),
        P("wide", "narrow", None),
        P("wide", None),
        P("wide", None),
        P("wide", None),
        P("wide", None),
        P(),
        P(),
        P(),
    )
    return jax.shard_map(body, mesh=mesh, in_specs=in_specs, out_specs=out_specs, check_vma=False)
```
